512 devices in a mesh: layer: 8 (over x, core), prow: 4 (over y), pcol: 16 (over z).
Axes of the slice: x: 4, y: 4, z: 16, core: 2. Of those that a mesh axis runs over, the one named last changes fastest.
Arguments:
- rhs: bfloat16 [8, 3, 16, 64, 128], P('layer', None, 'prow'), may hold values from -6 to 6
- diag_low: bfloat16 [8, 3, 16, 128, 128], P('layer', None, 'prow'), may hold values from -1 to 2
- diag_up: bfloat16 [8, 3, 16, 128, 128], P('layer', None, 'pcol'), may hold values from -1 to 2
- low_blocks: bfloat16 [8, 2, 16, 16, 128, 128], P('layer', None, 'prow', 'pcol'), may hold values from -0.1875 to 0.1875
- up_blocks: bfloat16 [8, 2, 16, 16, 128, 128], P('layer', None, 'prow', 'pcol'), may hold values from -0.1875 to 0.1875
- pattern: int32 [8, 2, 16, 16], P('layer', None, 'prow', 'pcol'), may hold values 0 or 1
- sub_sizes: int32 [8, 3, 16], P('layer'), may hold values from 32 to 128
- anc_rhs: bfloat16 [16, 64, 128], P('prow'), may hold values from -6 to 6
- anc_dl: bfloat16 [16, 128, 128], P('prow'), may hold values from -1 to 2
- anc_du: bfloat16 [16, 128, 128], P('prow'), may hold values from -1 to 2
- anc_low: bfloat16 [8, 16, 16, 128, 128], P('layer', 'prow', 'pcol'), may hold values from -0.0625 to 0.0625
- anc_up: bfloat16 [8, 16, 16, 128, 128], P('layer', 'prow', 'pcol'), may hold values from -0.1875 to 0.1875
- anc_pattern: int32 [8, 16, 16], P('layer', 'prow', 'pcol'), may hold values 0 or 1
Outputs:
- solution: bfloat16 [8, 3, 16, 64, 128], P('layer', None, 'pcol')
- anc_solution: bfloat16 [16, 64, 128], P('prow')
The draws below stay inside these ranges and needn't reach their ends.
All inputs are finite; a program needn't handle non-finite values. No bound on the sum of `pattern` or of `anc_pattern` on one device may be relied on, other than what follows from the above.
Results may differ from the reference program's by a relative error of at most 0.019.
Values may be sent and summed in bfloat16 or wider, within the bound.
A program may use at most 64 MiB of HBM per device.

```python
import math
import jax
import jax.numpy as jnp
from jax import lax

S = 128
R = 64
LEVELS = 3
W = 16
ANC = 16
N_LAYER = 8


def with_diagonal(key_diag, perturb, spread):
    diagonal = jax.random.uniform(key_diag, perturb.shape[:-1] + (1,), jnp.float32, 1.0 - spread, 1.0 + spread)
    return diagonal * jnp.eye(S, dtype=jnp.float32) + jnp.clip(perturb, -0.5, 0.5)


def draw_diag_low(key, part):
    key = jax.random.fold_in(key, 11)
    key_noise, key_diag = jax.random.split(key)
    dims = (N_LAYER, LEVELS, W, S, S)
    perturb = jax.random.normal(key_noise, dims, jnp.float32) * (0.6 / math.sqrt(S))
    return with_diagonal(key_diag, perturb, 0.4).astype(jnp.bfloat16)


def draw_diag_up(key, part):
    key = jax.random.fold_in(key, 23)
    key_noise, key_diag = jax.random.split(key)
    dims = (N_LAYER, LEVELS, W, S, S)
    perturb = jax.random.normal(key_noise, dims, jnp.float32) * (0.6 / math.sqrt(S))
    return with_diagonal(key_diag, perturb, 0.4).astype(jnp.bfloat16)


def draw_anc_dl(key, part):
    key = jax.random.fold_in(key, 37)
    key_noise, key_diag = jax.random.split(key)
    dims = (ANC, S, S)
    perturb = jax.random.normal(key_noise, dims, jnp.float32) * (0.6 / math.sqrt(S))
    return with_diagonal(key_diag, perturb, 0.4).astype(jnp.bfloat16)


def draw_anc_du(key, part):
    key = jax.random.fold_in(key, 41)
    key_noise, key_diag = jax.random.split(key)
    dims = (ANC, S, S)
    perturb = jax.random.normal(key_noise, dims, jnp.float32) * (0.6 / math.sqrt(S))
    return with_diagonal(key_diag, perturb, 0.4).astype(jnp.bfloat16)


def set_ends(result, rng, low, top_value):
    spot = [jax.random.randint(jax.random.fold_in(rng, axis), (), 0, length) for axis, length in enumerate(result.shape)]
    longest = result.shape.index(max(result.shape))
    beside = spot[:longest] + [(spot[longest] + 1) % result.shape[longest]] + spot[longest + 1:]
    return result.at[tuple(spot)].set(low).at[tuple(beside)].set(top_value)


def block_levels(own_key, extent, shards, low, high):
    def one(axis_at, parts):
        draws = jax.random.uniform(jax.random.fold_in(jax.random.fold_in(own_key, 6), axis_at), (parts,), jnp.float32, low / len(shards), high / len(shards))
        return jnp.repeat(jnp.exp(draws), extent[axis_at] // parts).reshape((-1,) + (1,) * (len(extent) - axis_at - 1))

    level = one(*shards[0])
    for cut in shards[1:]:
        level = level * one(*cut)
    return level


def gaussian(rng, shape, scale, most, pieces=(), held_as=jnp.bfloat16):
    drawn = jax.random.normal(rng, shape, jnp.float32) * scale
    if len(pieces) > 0:
        drawn = block_levels(rng, shape, pieces, -0.22, 0.18) * drawn
    return jnp.clip(drawn, min=-most, max=most).astype(held_as)


def setup_inputs(seed: int = 0) -> dict:
    arg_keys = jax.random.split(jax.random.key(seed), 14)
    rhs = gaussian(arg_keys[0], (N_LAYER, LEVELS, W, R, S), 1.0, 6.0, ((0, 8), (2, 4)))
    diag_low = draw_diag_low(jax.random.fold_in(arg_keys[13], 71), 0)
    diag_up = draw_diag_up(jax.random.fold_in(arg_keys[13], 71), 0)
    low_blocks = gaussian(arg_keys[3], (N_LAYER, LEVELS - 1, W, W, S, S), (S * W // 2) ** -0.5, 0.1875, ((0, 8), (2, 4), (3, 16)))
    up_blocks = gaussian(arg_keys[4], (N_LAYER, LEVELS - 1, W, W, S, S), (S * W // 2) ** -0.5, 0.1875, ((0, 8), (2, 4), (3, 16)))
    pattern = set_ends((jax.random.randint(arg_keys[5], (N_LAYER, LEVELS - 1, W, W), 0, 2) < 1).astype(jnp.int32), jax.random.fold_in(arg_keys[5], 1), 0, 1)
    sub_sizes = set_ends(jax.random.randint(arg_keys[6], (N_LAYER, LEVELS, W), S // 4, S + 1), jax.random.fold_in(arg_keys[6], 1), S // 4, S).astype(jnp.int32)
    anc_rhs = gaussian(arg_keys[7], (ANC, R, S), 1.0, 6.0, ((0, 4),))
    anc_dl = draw_anc_dl(jax.random.fold_in(arg_keys[13], 71), 0)
    anc_du = draw_anc_du(jax.random.fold_in(arg_keys[13], 71), 0)
    anc_low = gaussian(arg_keys[10], (N_LAYER, ANC, W, S, S), (S * W * N_LAYER // 2) ** -0.5, 0.0625, ((0, 8), (1, 4), (2, 16)))
    anc_up = gaussian(arg_keys[11], (N_LAYER, ANC, W, S, S), (S * ANC // 2) ** -0.5, 0.1875, ((0, 8), (1, 4), (2, 16)))
    anc_pattern = set_ends((jax.random.randint(arg_keys[12], (N_LAYER, ANC, W), 0, 2) < 1).astype(jnp.int32), jax.random.fold_in(arg_keys[12], 1), 0, 1)
    return {"rhs": rhs, "diag_low": diag_low, "diag_up": diag_up, "low_blocks": low_blocks, "up_blocks": up_blocks, "pattern": pattern, "sub_sizes": sub_sizes, "anc_rhs": anc_rhs, "anc_dl": anc_dl, "anc_du": anc_du, "anc_low": anc_low, "anc_up": anc_up, "anc_pattern": anc_pattern}


def rounded_difference(known, partial_value):
    lowered = (known.astype(jnp.float32) - partial_value).astype(jnp.bfloat16)
    return lax.optimization_barrier(lowered).astype(jnp.float32)


def apply_inverse(known, partial_value, inverse, live_mask):
    solved = jnp.einsum("irs,ist->irt", rounded_difference(known, partial_value), inverse.astype(jnp.float32))
    return jnp.where(live_mask, solved, 0.0).astype(jnp.bfloat16)


def child_sums(segments, blocks, links):
    products = jnp.einsum("jrs,ijst->ijrt", segments.astype(jnp.float32), blocks.astype(jnp.float32))
    return jnp.sum(products * links.astype(jnp.float32)[:, :, None, None], axis=1)


def parent_sums(segments, blocks, links):
    products = jnp.einsum("irs,ijst->ijrt", segments.astype(jnp.float32), blocks.astype(jnp.float32))
    return jnp.sum(products * links.astype(jnp.float32)[:, :, None, None], axis=0)


def reference(rhs, diag_low, diag_up, low_blocks, up_blocks, pattern, sub_sizes, anc_rhs, anc_dl, anc_du, anc_low, anc_up, anc_pattern):
    positions = jnp.arange(S, dtype=jnp.int32)
    live_all = positions[None, None, None, None, :] < sub_sizes[:, :, :, None, None]

    def forward_layer(operands):
        known, inverse, blocks, links, live_mask, anc_blocks, anc_links = operands
        solved_rows = []
        partial_value = jnp.zeros(known.shape[1:], jnp.float32)
        for level_index in range(LEVELS):
            if level_index > 0:
                partial_value = child_sums(solved_rows[-1], blocks[level_index - 1], links[level_index - 1])
            solved_rows.append(apply_inverse(known[level_index], partial_value, inverse[level_index], live_mask[level_index]))
        return jnp.stack(solved_rows), child_sums(solved_rows[-1], anc_blocks, anc_links)

    forward_rows, anc_parts = lax.map(forward_layer, (rhs, diag_low, low_blocks, pattern, live_all, anc_low, anc_pattern))
    anc_total = jnp.sum(anc_parts, axis=0)
    anc_forward = apply_inverse(anc_rhs, anc_total, anc_dl, True)
    anc_solution = apply_inverse(anc_forward, jnp.zeros(anc_total.shape, jnp.float32), anc_du, True)

    def backward_layer(operands):
        forward_known, inverse, blocks, links, live_mask, anc_blocks, anc_links = operands
        columns = [None] * LEVELS
        parent_rows = anc_solution
        for level_index in reversed(range(LEVELS)):
            if level_index == LEVELS - 1:
                partial_value = parent_sums(parent_rows, anc_blocks, anc_links)
            else:
                partial_value = parent_sums(parent_rows, blocks[level_index], links[level_index])
            columns[level_index] = apply_inverse(forward_known[level_index], partial_value, inverse[level_index], live_mask[level_index])
            parent_rows = columns[level_index]
        return jnp.stack(columns)

    solution = lax.map(backward_layer, (forward_rows, diag_up, up_blocks, pattern, live_all, anc_up, anc_pattern))
    return solution, anc_solution
```

```python
import functools

import jax
import jax.numpy as jnp
from jax import lax
from jax.experimental import pallas as pl
from jax.experimental.pallas import tpu as pltpu
from jax.sharding import PartitionSpec as P

MESH = pl.DeviceIdType.MESH
BF16 = jnp.bfloat16
F32 = jnp.float32


def far_first(n):
    return sorted(range(1, n), key=lambda d: (-min(d, n - d), d))


def dot(a, b):
    return jnp.dot(a, b, preferred_element_type=F32)


def kernel(
    nl, ny, nz, levels, rows, rq, S,
    rhs, diag_low, diag_up, low, up, pattern, sizes,
    anc_rhs, anc_dl, anc_du, anc_low, anc_up, anc_pattern,
    osol, oanc,
    pat_v, apat_v, size_v, raw, dmine, rfull, f0, dup, quarter,
    fset, bset,
    fsrc, frecv, lrecv, ag, final,
    in_sem, own_sem, far_sem, set_send, set_recv, one_send, one_recv,
    fs_sem, fr_sem, l_send, l_recv, ag_send, ag_recv, oa_send, oa_recv, os_send, os_recv,
):
    k = lax.axis_index("layer")
    p = lax.axis_index("prow")
    c = lax.axis_index("pcol")
    j = lax.rem(c, rows)
    owner = p == c // rows
    nset = 2 * levels
    y_order, z_order, l_order = far_first(ny), far_first(nz), far_first(nl)

    def y_peer(d):
        return (k, lax.rem(p + d, ny), c)

    def z_peer(d):
        return (k, p, lax.rem(c + d, nz))

    def l_peer(d):
        return (lax.rem(k + d, nl), p, c)

    def drain(ref, sem):
        pltpu.make_async_copy(ref, ref, sem).wait()

    def remote(src, dst, send, recv, device):
        return pltpu.make_async_remote_copy(
            src_ref=src, dst_ref=dst, send_sem=send, recv_sem=recv,
            device_id=device, device_id_type=MESH,
        )

    reach = nz // 4
    near = [d for d in z_order if min(d, nz - d) <= reach]
    barrier = pltpu.get_barrier_semaphore()
    greeted = [z_peer(d) for d in near] + [y_peer(d) for d in y_order] + [l_peer(d) for d in l_order]
    for device in greeted:
        pl.semaphore_signal(barrier, inc=1, device_id=device, device_id_type=MESH)

    def fetch(src, dst, n):
        copy = pltpu.make_async_copy(src, dst, in_sem.at[n])
        copy.start()
        return copy

    sets_in = [low.at[0, l, :, 0] for l in range(levels - 1)] + [anc_low.at[0, :, 0], anc_up.at[0, :, 0]]
    sets_in += [up.at[0, l, :, 0] for l in reversed(range(levels - 1))]
    got_pat = fetch(pattern, pat_v, 0)
    got_apat = fetch(anc_pattern, apat_v, 1)
    got_size = fetch(sizes, size_v, 2)
    got_sets = [fetch(sets_in[0], raw.at[0], 3)]
    own = [
        pltpu.make_async_copy(diag_low.at[0, :, j], dmine.at[pl.ds(0, levels)], own_sem.at[0]),
        pltpu.make_async_copy(rhs.at[0, :, j], rfull.at[pl.ds(0, levels)], own_sem.at[1]),
        pltpu.make_async_copy(anc_rhs.at[j], rfull.at[levels], own_sem.at[2]),
        pltpu.make_async_copy(anc_dl.at[j], dmine.at[levels], own_sem.at[3]),
        pltpu.make_async_copy(anc_du.at[j], dmine.at[levels + 1], own_sem.at[4]),
    ]

    @pl.when(owner)
    def _():
        for copy in own:
            copy.start()

    for n in range(1, nset):
        got_sets.append(fetch(sets_in[n], raw.at[n], 3 + n))
    got_dup = fetch(diag_up.at[0, :, 0], dup, 3 + nset)

    def link(n, i):
        if n < levels - 1:
            return pat_v[0, n, i, 0]
        if n < levels + 1:
            return apat_v[0, i, 0]
        return pat_v[0, nset - 1 - n, i, 0]

    def mask_set(n):
        got_sets[n].wait()
        for i in range(rows):
            present = jnp.full((S, S), link(n, i), jnp.int32).astype(F32).astype(BF16)
            block = raw[n, i] * present
            if n < levels:
                fset[n, p, :, i * S:(i + 1) * S] = block
            else:
                bset[n - levels, p, i * S:(i + 1) * S, :] = block

    set_copies = []

    def send_set(n):
        part = fset.at[n, p] if n < levels else bset.at[n - levels, p]
        for m, d in enumerate(y_order):
            copy = remote(part, part, set_send.at[n, m], set_recv.at[n], y_peer(d))
            copy.start()
            set_copies.append(copy)

    def wait_set(n):
        whole = fset.at[n] if n < levels else bset.at[n - levels]
        drain(whole.at[pl.ds(0, ny - 1)], set_recv.at[n])

    def live(level, value):
        columns = lax.broadcasted_iota(jnp.int32, value.shape, 1)
        return jnp.where(columns < size_v[0, level, c], value, 0.0).astype(BF16)

    got_pat.wait()
    got_apat.wait()
    got_size.wait()
    mask_set(0)

    @pl.when(owner)
    def _():
        for copy in own[:3]:
            copy.wait()
        f0[...] = live(0, dot(rfull[0], dmine[0]))
        mine = pl.ds(pl.multiple_of(p * rq, rq), rq)
        quarter[0] = f0[mine]
        for n in range(levels):
            quarter[n + 1] = rfull[n + 1, mine]

    pl.semaphore_wait(barrier, len(greeted))
    for d in (reach, nz - reach):
        pl.semaphore_signal(far_sem, inc=1, device_id=z_peer(d), device_id_type=MESH)

    def one_copies(m, d):
        theirs = pl.ds(pl.multiple_of(lax.rem(p + d, ny) * rq, rq), rq)
        pairs = [
            (f0.at[theirs], quarter.at[0]),
            (rfull.at[pl.ds(1, levels), theirs], quarter.at[pl.ds(1, levels)]),
            (dmine.at[1], dmine.at[1]),
            (dmine.at[pl.ds(2, levels)], dmine.at[pl.ds(2, levels)]),
        ]
        return [
            remote(src, dst, one_send.at[n, m], one_recv.at[n], y_peer(d))
            for n, (src, dst) in enumerate(pairs)
        ]

    one_all = [one_copies(m, d) for m, d in enumerate(y_order)]

    def send_one(n):
        @pl.when(owner)
        def _():
            for copies in one_all:
                copies[n].start()

    def wait_one(n):
        @pl.when(jnp.logical_not(owner))
        def _():
            one_all[0][n].wait_recv()

    send_one(0)
    send_set(0)
    send_one(1)
    send_one(2)
    mask_set(1)
    send_set(1)

    @pl.when(owner)
    def _():
        for copy in own[3:]:
            copy.wait()

    send_one(3)
    for n in range(2, nset):
        mask_set(n)
        send_set(n)

    segment = None
    forward = []
    for level in range(levels + 1):
        if level == 0:
            wait_one(0)
            segment = quarter[0]
            forward.append(segment)
            continue
        n = level - 1
        wait_set(n)
        for s in range(ny):
            product = dot(segment, fset[n, s])
            for i in range(rows):
                fsrc[n, s * rows + i] = product[:, i * S:(i + 1) * S].astype(BF16)
        if n == 0:
            pl.semaphore_wait(far_sem, 2)
        for d in z_order:
            target = lax.rem(c + d, nz)
            remote(fsrc.at[n, target], frecv.at[n, d - 1], fs_sem.at[n], fr_sem.at[n], z_peer(d)).start()
        if level == 1:
            wait_one(1)
            wait_one(2)
        if level == 2:
            wait_one(3)
        drain(frecv.at[n], fr_sem.at[n])
        total = fsrc[n, c].astype(F32)
        for d in range(1, nz):
            total = total + frecv[n, d - 1].astype(F32)
        if level < levels:
            lowered = (quarter[level].astype(F32) - total).astype(BF16)
            segment = live(level, dot(lowered, dmine[level]))
            forward.append(segment)

    lrecv[k] = total.astype(BF16)
    for d in l_order:
        remote(lrecv.at[k], lrecv.at[k], l_send, l_recv, l_peer(d)).start()
    drain(lrecv.at[pl.ds(0, nl - 1)], l_recv)
    total = lrecv[0].astype(F32)
    for n in range(1, nl):
        total = total + lrecv[n].astype(F32)
    lowered = (quarter[levels].astype(F32) - total).astype(BF16)
    afwd = dot(lowered, dmine[levels]).astype(BF16)
    solved = dot(afwd, dmine[levels + 1]).astype(BF16)

    mine = pl.ds(pl.multiple_of(p * rq, rq), rq)
    got_dup.wait()
    sol_copies = []
    anc_copies = []
    for step in range(levels + 1):
        level = levels - step
        if level < levels:
            osol[0, level, 0, mine] = solved
            part = osol.at[0, level, 0, mine]
            for m, d in enumerate(y_order):
                copy = remote(part, part, os_send.at[level, m], os_recv.at[level], y_peer(d))
                copy.start()
                sol_copies.append(copy)
        if level == 0:
            break
        ag[step, c] = solved
        for d in z_order:
            remote(ag.at[step, c], ag.at[step, c], ag_send.at[step], ag_recv.at[step], z_peer(d)).start()
        wait_set(levels + step)
        drain(ag.at[step, pl.ds(0, nz - 1)], ag_recv.at[step])
        if step == 0:
            for i in range(rows):
                oanc[i, mine] = ag[0, p * rows + i]
                for m, d in enumerate(y_order):
                    theirs = lax.rem(p + d, ny) * rows + i
                    copy = remote(ag.at[0, theirs], oanc.at[i, mine], oa_send.at[i, m], oa_recv, y_peer(d))
                    copy.start()
                    anc_copies.append(copy)
        total = None
        for s in range(ny):
            parents = jnp.concatenate([ag[step, s * rows + i] for i in range(rows)], axis=1)
            product = dot(parents, bset[step, s])
            total = product if total is None else total + product
        below = level - 1
        lowered = (forward[below].astype(F32) - total).astype(BF16)
        solved = live(below, dot(lowered, dup[below]))

    for level in reversed(range(levels)):
        drain(osol.at[0, level, 0, pl.ds(0, (ny - 1) * rq)], os_recv.at[level])
    drain(oanc.at[:, pl.ds(0, (ny - 1) * rq)], oa_recv)
    for copy in set_copies + sol_copies + anc_copies:
        copy.wait_send()

    @pl.when(owner)
    def _():
        for copies in one_all:
            for copy in copies:
                copy.wait_send()

    for n in range(levels):
        drain(frecv.at[n], fs_sem.at[n])
        drain(ag.at[n, pl.ds(0, nz - 1)], ag_send.at[n])
    drain(lrecv.at[pl.ds(0, nl - 1)], l_send)


def per_device(nl, ny, nz, *operands):
    rhs, diag_low = operands[0], operands[1]
    anc_rhs = operands[7]
    levels, rows, R, S = rhs.shape[1:]
    rq = R // ny
    nset = 2 * levels
    dma = pltpu.SemaphoreType.DMA
    scratch = [
        pltpu.SMEM(operands[5].shape, jnp.int32),
        pltpu.SMEM(operands[12].shape, jnp.int32),
        pltpu.SMEM(operands[6].shape, jnp.int32),
        pltpu.VMEM((nset, rows, S, S), BF16),
        pltpu.VMEM((levels + 2, S, S), BF16),
        pltpu.VMEM((levels + 1, R, S), BF16),
        pltpu.VMEM((R, S), BF16),
        pltpu.VMEM((levels, S, S), BF16),
        pltpu.VMEM((levels + 1, rq, S), BF16),
        pltpu.VMEM((levels, ny, S, rows * S), BF16),
        pltpu.VMEM((levels, ny, rows * S, S), BF16),
        pltpu.VMEM((levels, nz, rq, S), BF16),
        pltpu.VMEM((levels, nz - 1, rq, S), BF16),
        pltpu.VMEM((nl, rq, S), BF16),
        pltpu.VMEM((levels, nz, rq, S), BF16),
        pltpu.VMEM((rq, S), BF16),
        dma((4 + nset,)), dma((5,)), pltpu.SemaphoreType.REGULAR,
        dma((nset, ny - 1)), dma((nset,)), dma((4, ny - 1)), dma((4,)),
        dma((levels,)), dma((levels,)), dma, dma, dma((levels,)), dma((levels,)),
        dma((rows, ny - 1)), dma, dma((levels, ny - 1)), dma((levels,)),
    ]
    return pl.pallas_call(
        functools.partial(kernel, nl, ny, nz, levels, rows, rq, S),
        out_shape=(
            jax.ShapeDtypeStruct((1, levels, 1, R, S), BF16),
            jax.ShapeDtypeStruct((rows, R, S), BF16),
        ),
        in_specs=[pl.BlockSpec(memory_space=pl.ANY)] * len(operands),
        out_specs=(pl.BlockSpec(memory_space=pltpu.VMEM),) * 2,
        scratch_shapes=scratch,
        compiler_params=pltpu.CompilerParams(
            collective_id=0, has_side_effects=True, vmem_limit_bytes=48 * 2**20
        ),
        name="solve",
    )(*operands)


def solution(mesh):
    sizes = [mesh.shape[name] for name in ("layer", "prow", "pcol")]
    return jax.shard_map(
        functools.partial(per_device, *sizes),
        mesh=mesh,
        in_specs=(
            P("layer", None, "prow", None, None),
            P("layer", None, "prow", None, None),
            P("layer", None, "pcol", None, None),
            P("layer", None, "prow", "pcol", None, None),
            P("layer", None, "prow", "pcol", None, None),
            P("layer", None, "prow", "pcol"),
            P("layer", None, None),
            P("prow", None, None),
            P("prow", None, None),
            P("prow", None, None),
            P("layer", "prow", "pcol", None, None),
            P("layer", "prow", "pcol", None, None),
            P("layer", "prow", "pcol"),
        ),
        out_specs=(P("layer", None, "pcol", None, None), P("prow", None, None)),
        check_vma=False,
    )
```

```python
import functools

import jax
import jax.numpy as jnp
from jax import lax
from jax.experimental import pallas as pl
from jax.experimental.pallas import tpu as pltpu
from jax.sharding import PartitionSpec as P

MESH = pl.DeviceIdType.MESH
BF16 = jnp.bfloat16
F32 = jnp.float32


def far_first(n):
    return sorted(range(1, n), key=lambda d: (-min(d, n - d), d))


def dot(a, b):
    return jnp.dot(a, b, preferred_element_type=F32)


def kernel(
    nl, ny, nz, levels, rows, rq, S,
    rhs, diag_low, diag_up, low, up, pattern, sizes,
    anc_rhs, anc_dl, anc_du, anc_low, anc_up, anc_pattern,
    osol, oanc,
    pat_v, apat_v, size_v, raw, dmine, rfull, f0, dup, quarter,
    fset, bset,
    fsrc, frecv, lrecv, ag, final,
    in_sem, own_sem, far_sem, set_send, set_recv, one_send, one_recv,
    fs_sem, fr_sem, l_send, l_recv, ag_send, ag_recv, oa_send, oa_recv, os_send, os_recv,
):
    k = lax.axis_index("layer")
    p = lax.axis_index("prow")
    c = lax.axis_index("pcol")
    j = lax.rem(c, rows)
    owner = p == c // rows
    nset = 2 * levels
    y_order, z_order, l_order = far_first(ny), far_first(nz), far_first(nl)

    def y_peer(d):
        return (k, lax.rem(p + d, ny), c)

    def z_peer(d):
        return (k, p, lax.rem(c + d, nz))

    def l_peer(d):
        return (lax.rem(k + d, nl), p, c)

    def drain(ref, sem):
        pltpu.make_async_copy(ref, ref, sem).wait()

    def remote(src, dst, send, recv, device):
        return pltpu.make_async_remote_copy(
            src_ref=src, dst_ref=dst, send_sem=send, recv_sem=recv,
            device_id=device, device_id_type=MESH,
        )

    reach = nz // 4
    near = [d for d in z_order if min(d, nz - d) <= reach]
    barrier = pltpu.get_barrier_semaphore()
    greeted = [z_peer(d) for d in near] + [y_peer(d) for d in y_order] + [l_peer(d) for d in l_order]
    for device in greeted:
        pl.semaphore_signal(barrier, inc=1, device_id=device, device_id_type=MESH)

    def fetch(src, dst, n):
        copy = pltpu.make_async_copy(src, dst, in_sem.at[n])
        copy.start()
        return copy

    sets_in = [low.at[0, l, :, 0] for l in range(levels - 1)] + [anc_low.at[0, :, 0], anc_up.at[0, :, 0]]
    sets_in += [up.at[0, l, :, 0] for l in reversed(range(levels - 1))]
    got_pat = fetch(pattern, pat_v, 0)
    got_apat = fetch(anc_pattern, apat_v, 1)
    got_size = fetch(sizes, size_v, 2)
    got_sets = [fetch(sets_in[0], raw.at[0], 3)]
    own = [
        pltpu.make_async_copy(diag_low.at[0, :, j], dmine.at[pl.ds(0, levels)], own_sem.at[0]),
        pltpu.make_async_copy(rhs.at[0, :, j], rfull.at[pl.ds(0, levels)], own_sem.at[1]),
        pltpu.make_async_copy(anc_rhs.at[j], rfull.at[levels], own_sem.at[2]),
        pltpu.make_async_copy(anc_dl.at[j], dmine.at[levels], own_sem.at[3]),
        pltpu.make_async_copy(anc_du.at[j], dmine.at[levels + 1], own_sem.at[4]),
    ]

    @pl.when(owner)
    def _():
        for copy in own:
            copy.start()

    for n in range(1, nset):
        got_sets.append(fetch(sets_in[n], raw.at[n], 3 + n))
    got_dup = fetch(diag_up.at[0, :, 0], dup, 3 + nset)

    def link(n, i):
        if n < levels - 1:
            return pat_v[0, n, 0, i]
        if n < levels + 1:
            return apat_v[0, 0, i]
        return pat_v[0, nset - 1 - n, 0, i]

    def mask_set(n):
        got_sets[n].wait()
        for i in range(rows):
            present = jnp.full((S, S), link(n, i), jnp.int32).astype(F32).astype(BF16)
            block = raw[n, i] * present
            if n < levels:
                fset[n, p, :, i * S:(i + 1) * S] = block
            else:
                bset[n - levels, p, i * S:(i + 1) * S, :] = block

    set_copies = []

    def send_set(n):
        part = fset.at[n, p] if n < levels else bset.at[n - levels, p]
        for m, d in enumerate(y_order):
            copy = remote(part, part, set_send.at[n, m], set_recv.at[n], y_peer(d))
            copy.start()
            set_copies.append(copy)

    def wait_set(n):
        whole = fset.at[n] if n < levels else bset.at[n - levels]
        drain(whole.at[pl.ds(0, ny - 1)], set_recv.at[n])

    def live(level, value):
        columns = lax.broadcasted_iota(jnp.int32, value.shape, 1)
        return jnp.where(columns < size_v[level, 0, c], value, 0.0).astype(BF16)

    got_pat.wait()
    got_apat.wait()
    got_size.wait()
    mask_set(0)

    @pl.when(owner)
    def _():
        for copy in own[:3]:
            copy.wait()
        f0[...] = live(0, dot(rfull[0], dmine[0]))
        mine = pl.ds(pl.multiple_of(p * rq, rq), rq)
        quarter[0] = f0[mine]
        for n in range(levels):
            quarter[n + 1] = rfull[n + 1, mine]

    pl.semaphore_wait(barrier, len(greeted))
    for d in (reach, nz - reach):
        pl.semaphore_signal(far_sem, inc=1, device_id=z_peer(d), device_id_type=MESH)

    def one_copies(m, d):
        theirs = pl.ds(pl.multiple_of(lax.rem(p + d, ny) * rq, rq), rq)
        pairs = [
            (f0.at[theirs], quarter.at[0]),
            (rfull.at[pl.ds(1, levels), theirs], quarter.at[pl.ds(1, levels)]),
            (dmine.at[1], dmine.at[1]),
            (dmine.at[pl.ds(2, levels)], dmine.at[pl.ds(2, levels)]),
        ]
        return [
            remote(src, dst, one_send.at[n, m], one_recv.at[n], y_peer(d))
            for n, (src, dst) in enumerate(pairs)
        ]

    one_all = [one_copies(m, d) for m, d in enumerate(y_order)]

    def send_one(n):
        @pl.when(owner)
        def _():
            for copies in one_all:
                copies[n].start()

    def wait_one(n):
        @pl.when(jnp.logical_not(owner))
        def _():
            one_all[0][n].wait_recv()

    send_one(0)
    send_set(0)
    send_one(1)
    send_one(2)
    mask_set(1)
    send_set(1)

    @pl.when(owner)
    def _():
        for copy in own[3:]:
            copy.wait()

    send_one(3)
    for n in range(2, nset):
        mask_set(n)
        send_set(n)

    segment = None
    forward = []
    for level in range(levels + 1):
        if level == 0:
            wait_one(0)
            segment = quarter[0]
            forward.append(segment)
            continue
        n = level - 1
        wait_set(n)
        for s in range(ny):
            product = dot(segment, fset[n, s])
            for i in range(rows):
                fsrc[n, s * rows + i] = product[:, i * S:(i + 1) * S].astype(BF16)
        if n == 0:
            pl.semaphore_wait(far_sem, 2)
        for d in z_order:
            target = lax.rem(c + d, nz)
            remote(fsrc.at[n, target], frecv.at[n, d - 1], fs_sem.at[n], fr_sem.at[n], z_peer(d)).start()
        if level == 1:
            wait_one(1)
            wait_one(2)
        if level == 2:
            wait_one(3)
        drain(frecv.at[n], fr_sem.at[n])
        total = fsrc[n, c].astype(F32)
        for d in range(1, nz):
            total = total + frecv[n, d - 1].astype(F32)
        if level < levels:
            lowered = (quarter[level].astype(F32) - total).astype(BF16)
            segment = live(level, dot(lowered, dmine[level]))
            forward.append(segment)

    lrecv[k] = total.astype(BF16)
    for d in l_order:
        remote(lrecv.at[k], lrecv.at[k], l_send, l_recv, l_peer(d)).start()
    drain(lrecv.at[pl.ds(0, nl - 1)], l_recv)
    total = lrecv[0].astype(F32)
    for n in range(1, nl):
        total = total + lrecv[n].astype(F32)
    lowered = (quarter[levels].astype(F32) - total).astype(BF16)
    afwd = dot(lowered, dmine[levels]).astype(BF16)
    solved = dot(afwd, dmine[levels + 1]).astype(BF16)

    mine = pl.ds(pl.multiple_of(p * rq, rq), rq)
    got_dup.wait()
    sol_copies = []
    anc_copies = []
    for step in range(levels + 1):
        level = levels - step
        if level < levels:
            osol[0, level, 0, mine] = solved
            part = osol.at[0, level, 0, mine]
            for m, d in enumerate(y_order):
                copy = remote(part, part, os_send.at[level, m], os_recv.at[level], y_peer(d))
                copy.start()
                sol_copies.append(copy)
        if level == 0:
            break
        ag[step, c] = solved
        for d in z_order:
            remote(ag.at[step, c], ag.at[step, c], ag_send.at[step], ag_recv.at[step], z_peer(d)).start()
        wait_set(levels + step)
        drain(ag.at[step, pl.ds(0, nz - 1)], ag_recv.at[step])
        if step == 0:
            for i in range(rows):
                oanc[i, mine] = ag[0, p * rows + i]
                for m, d in enumerate(y_order):
                    theirs = lax.rem(p + d, ny) * rows + i
                    copy = remote(ag.at[0, theirs], oanc.at[i, mine], oa_send.at[i, m], oa_recv, y_peer(d))
                    copy.start()
                    anc_copies.append(copy)
        total = None
        for s in range(ny):
            parents = jnp.concatenate([ag[step, s * rows + i] for i in range(rows)], axis=1)
            product = dot(parents, bset[step, s])
            total = product if total is None else total + product
        below = level - 1
        lowered = (forward[below].astype(F32) - total).astype(BF16)
        solved = live(below, dot(lowered, dup[below]))

    for level in reversed(range(levels)):
        drain(osol.at[0, level, 0, pl.ds(0, (ny - 1) * rq)], os_recv.at[level])
    drain(oanc.at[:, pl.ds(0, (ny - 1) * rq)], oa_recv)
    for copy in set_copies + sol_copies + anc_copies:
        copy.wait_send()

    @pl.when(owner)
    def _():
        for copies in one_all:
            for copy in copies:
                copy.wait_send()

    for n in range(levels):
        drain(frecv.at[n], fs_sem.at[n])
        drain(ag.at[n, pl.ds(0, nz - 1)], ag_send.at[n])
    drain(lrecv.at[pl.ds(0, nl - 1)], l_send)


def per_device(nl, ny, nz, *operands):
    operands = list(operands)
    operands[5] = operands[5].transpose(0, 1, 3, 2)
    operands[6] = operands[6].transpose(1, 0, 2)
    operands[12] = operands[12].transpose(0, 2, 1)
    rhs = operands[0]
    levels, rows, R, S = rhs.shape[1:]
    rq = R // ny
    nset = 2 * levels
    dma = pltpu.SemaphoreType.DMA
    scratch = [
        pltpu.SMEM(operands[5].shape, jnp.int32),
        pltpu.SMEM(operands[12].shape, jnp.int32),
        pltpu.SMEM(operands[6].shape, jnp.int32),
        pltpu.VMEM((nset, rows, S, S), BF16),
        pltpu.VMEM((levels + 2, S, S), BF16),
        pltpu.VMEM((levels + 1, R, S), BF16),
        pltpu.VMEM((R, S), BF16),
        pltpu.VMEM((levels, S, S), BF16),
        pltpu.VMEM((levels + 1, rq, S), BF16),
        pltpu.VMEM((levels, ny, S, rows * S), BF16),
        pltpu.VMEM((levels, ny, rows * S, S), BF16),
        pltpu.VMEM((levels, nz, rq, S), BF16),
        pltpu.VMEM((levels, nz - 1, rq, S), BF16),
        pltpu.VMEM((nl, rq, S), BF16),
        pltpu.VMEM((levels, nz, rq, S), BF16),
        pltpu.VMEM((rq, S), BF16),
        dma((4 + nset,)), dma((5,)), pltpu.SemaphoreType.REGULAR,
        dma((nset, ny - 1)), dma((nset,)), dma((4, ny - 1)), dma((4,)),
        dma((levels,)), dma((levels,)), dma, dma, dma((levels,)), dma((levels,)),
        dma((rows, ny - 1)), dma, dma((levels, ny - 1)), dma((levels,)),
    ]
    return pl.pallas_call(
        functools.partial(kernel, nl, ny, nz, levels, rows, rq, S),
        out_shape=(
            jax.ShapeDtypeStruct((1, levels, 1, R, S), BF16),
            jax.ShapeDtypeStruct((rows, R, S), BF16),
        ),
        in_specs=[pl.BlockSpec(memory_space=pl.ANY)] * len(operands),
        out_specs=(pl.BlockSpec(memory_space=pltpu.VMEM),) * 2,
        scratch_shapes=scratch,
        compiler_params=pltpu.CompilerParams(
            collective_id=0, has_side_effects=True, vmem_limit_bytes=60 * 2**20
        ),
        name="solve",
    )(*operands)


def solution(mesh):
    sizes = [mesh.shape[name] for name in ("layer", "prow", "pcol")]
    return jax.shard_map(
        functools.partial(per_device, *sizes),
        mesh=mesh,
        in_specs=(
            P("layer", None, "prow", None, None),
            P("layer", None, "prow", None, None),
            P("layer", None, "pcol", None, None),
            P("layer", None, "prow", "pcol", None, None),
            P("layer", None, "prow", "pcol", None, None),
            P("layer", None, "prow", "pcol"),
            P("layer", None, None),
            P("prow", None, None),
            P("prow", None, None),
            P("prow", None, None),
            P("layer", "prow", "pcol", None, None),
            P("layer", "prow", "pcol", None, None),
            P("layer", "prow", "pcol"),
        ),
        out_specs=(P("layer", None, "pcol", None, None), P("prow", None, None)),
        check_vma=False,
    )
```

```python
import functools

import jax
import jax.numpy as jnp
from jax import lax
from jax.experimental import pallas as pl
from jax.experimental.pallas import tpu as pltpu
from jax.sharding import PartitionSpec as P

MESH = pl.DeviceIdType.MESH
BF16 = jnp.bfloat16
F32 = jnp.float32


def far_first(n):
    return sorted(range(1, n), key=lambda d: (-min(d, n - d), d))


def dot(a, b):
    return jnp.dot(a, b, preferred_element_type=F32)


def kernel(
    nl, ny, nz, levels, rows, rq, S,
    rhs, diag_low, diag_up, low, up, pattern, sizes,
    anc_rhs, anc_dl, anc_du, anc_low, anc_up, anc_pattern,
    osol, oanc,
    pat_v, apat_v, size_v, raw, dmine, rfull, f0, dup, quarter,
    fset, bset,
    fsrc, frecv, lrecv, ag, wg, ring, eacc,
    in_sem, own_sem, far_sem, set_send, set_recv, one_send, one_recv,
    fs_sem, fr_sem, l_send, l_recv, ag_send, ag_recv, oa_send, oa_recv, os_send, os_recv,
    w_send, w_recv, ring_send, ring_recv,
):
    k = lax.axis_index("layer")
    p = lax.axis_index("prow")
    c = lax.axis_index("pcol")
    j = lax.rem(c, rows)
    owner = p == c // rows
    nset = 2 * levels
    composed = nset
    ring_steps = nz // 2
    half = rows * S // 2
    y_order, z_order, l_order = far_first(ny), far_first(nz), far_first(nl)

    def y_peer(d):
        return (k, lax.rem(p + d, ny), c)

    def z_peer(d):
        return (k, p, lax.rem(c + d, nz))

    def l_peer(d):
        return (lax.rem(k + d, nl), p, c)

    def drain(ref, sem):
        pltpu.make_async_copy(ref, ref, sem).wait()

    def remote(src, dst, send, recv, device):
        return pltpu.make_async_remote_copy(
            src_ref=src, dst_ref=dst, send_sem=send, recv_sem=recv,
            device_id=device, device_id_type=MESH,
        )

    reach = nz // 4
    near = [d for d in z_order if min(d, nz - d) <= reach]
    barrier = pltpu.get_barrier_semaphore()
    greeted = [z_peer(d) for d in near] + [y_peer(d) for d in y_order] + [l_peer(d) for d in l_order]
    for device in greeted:
        pl.semaphore_signal(barrier, inc=1, device_id=device, device_id_type=MESH)

    def fetch(src, dst, n):
        copy = pltpu.make_async_copy(src, dst, in_sem.at[n])
        copy.start()
        return copy

    sets_in = [low.at[0, l, :, 0] for l in range(levels - 1)] + [anc_low.at[0, :, 0], anc_up.at[0, :, 0]]
    sets_in += [up.at[0, l, :, 0] for l in reversed(range(levels - 1))]
    got_pat = fetch(pattern, pat_v, 0)
    got_apat = fetch(anc_pattern, apat_v, 1)
    got_size = fetch(sizes, size_v, 2)
    got_sets = [fetch(sets_in[0], raw.at[0], 3)]
    own = [
        pltpu.make_async_copy(diag_low.at[0, :, j], dmine.at[pl.ds(0, levels)], own_sem.at[0]),
        pltpu.make_async_copy(rhs.at[0, :, j], rfull.at[pl.ds(0, levels)], own_sem.at[1]),
        pltpu.make_async_copy(anc_rhs.at[j], rfull.at[levels], own_sem.at[2]),
        pltpu.make_async_copy(anc_dl.at[j], dmine.at[levels], own_sem.at[3]),
        pltpu.make_async_copy(anc_du.at[j], dmine.at[levels + 1], own_sem.at[4]),
    ]

    @pl.when(owner)
    def _():
        for copy in own:
            copy.start()

    for n in range(1, nset):
        got_sets.append(fetch(sets_in[n], raw.at[n], 3 + n))
    got_dup = fetch(diag_up.at[0, :, 0], dup, 3 + nset)

    def link(n, i):
        if n < levels - 1:
            return pat_v[0, n, 0, i]
        if n < levels + 1:
            return apat_v[0, 0, i]
        return pat_v[0, nset - 1 - n, 0, i]

    def mask_set(n):
        got_sets[n].wait()
        for i in range(rows):
            present = jnp.full((S, S), link(n, i), jnp.int32).astype(F32).astype(BF16)
            block = raw[n, i] * present
            if n < levels:
                fset[n, p, :, i * S:(i + 1) * S] = block
            else:
                bset[n - levels, p, i * S:(i + 1) * S, :] = block

    set_copies = []

    def send_set(n):
        part = fset.at[n, p] if n < levels else bset.at[n - levels, p]
        for m, d in enumerate(y_order):
            copy = remote(part, part, set_send.at[n, m], set_recv.at[n], y_peer(d))
            copy.start()
            set_copies.append(copy)

    def wait_set(n):
        whole = fset.at[n] if n < levels else bset.at[n - levels]
        drain(whole.at[pl.ds(0, ny - 1)], set_recv.at[n])

    def live(level, value):
        columns = lax.broadcasted_iota(jnp.int32, value.shape, 1)
        return jnp.where(columns < size_v[level, 0, c], value, 0.0).astype(BF16)

    def ring_parts(t, h, move):
        both = [(0, lax.rem(c + nz - t - move, nz), 1), (1, lax.rem(c + t + move, nz), nz - 1)]
        return [both[h]] if t == ring_steps - 1 else both

    ring_copies = []

    def ring_start(t, h):
        for m, slot, d in ring_parts(t, h, 0):
            block = ring.at[slot, pl.ds(h * half, half)]
            copy = remote(block, block, ring_send.at[m, h, t], ring_recv.at[m, h, t], z_peer(d))
            copy.start()
            ring_copies.append(copy)

    def ring_pass(t):
        for h in range(2):
            for m, slot, d in ring_parts(t, h, 1):
                drain(ring.at[slot, pl.ds(h * half, half)], ring_recv.at[m, h, t])
            if t + 1 < ring_steps:
                ring_start(t + 1, h)

    def up0(slot):
        row = pl.ds(pl.multiple_of(lax.rem(slot, rows) * S, S), S)
        return bset[levels - 1, slot // rows, row, :]

    def compose(offsets):
        slots = [lax.rem(c + o, nz) for o in offsets]
        left = jnp.concatenate([ring[slot] for slot in slots], axis=1)
        right = jnp.concatenate([up0(slot) for slot in slots], axis=0)
        eacc[...] += dot(left, right)

    got_pat.wait()
    got_apat.wait()
    got_size.wait()
    mask_set(0)

    @pl.when(owner)
    def _():
        for copy in own[:3]:
            copy.wait()
        f0[...] = live(0, dot(rfull[0], dmine[0]))
        mine = pl.ds(pl.multiple_of(p * rq, rq), rq)
        quarter[0] = f0[mine]
        for n in range(levels):
            quarter[n + 1] = rfull[n + 1, mine]

    eacc[...] = jnp.zeros_like(eacc)
    mask_set(levels + 1)
    got_dup.wait()
    ring[c] = live(1, dot(bset[1, p], dup[1]))
    pl.semaphore_wait(barrier, len(greeted))
    for d in (reach, nz - reach):
        pl.semaphore_signal(far_sem, inc=1, device_id=z_peer(d), device_id_type=MESH)

    def one_copies(m, d):
        theirs = pl.ds(pl.multiple_of(lax.rem(p + d, ny) * rq, rq), rq)
        pairs = [
            (f0.at[theirs], quarter.at[0]),
            (rfull.at[pl.ds(1, levels), theirs], quarter.at[pl.ds(1, levels)]),
            (dmine.at[1], dmine.at[1]),
            (dmine.at[pl.ds(2, levels)], dmine.at[pl.ds(2, levels)]),
        ]
        return [
            remote(src, dst, one_send.at[n, m], one_recv.at[n], y_peer(d))
            for n, (src, dst) in enumerate(pairs)
        ]

    one_all = [one_copies(m, d) for m, d in enumerate(y_order)]

    def send_one(n):
        @pl.when(owner)
        def _():
            for copies in one_all:
                copies[n].start()

    def wait_one(n):
        @pl.when(jnp.logical_not(owner))
        def _():
            one_all[0][n].wait_recv()

    send_one(0)
    send_set(0)
    ring_start(0, 0)
    ring_start(0, 1)
    send_one(1)
    send_one(2)
    mask_set(1)
    send_set(1)

    @pl.when(owner)
    def _():
        for copy in own[3:]:
            copy.wait()

    send_one(3)

    for n in [2, nset - 1, levels, levels + 1]:
        if n != levels + 1:
            mask_set(n)
        send_set(n)
    ring_pass(0)
    if ring_steps > 1:
        ring_pass(1)

    plan = {
        1: [("step", 2)],
        2: [("step", 3)],
        3: [("step", 4), ("add", 1), ("add", 2), ("add", 3), ("add", 4)],
        4: [("step", 5)],
        5: [("step", 6), ("add", 5), ("add", 6), ("step", 7), ("add", 7)],
    }

    def background(phase):
        for what, n in plan[phase]:
            if what == "step" and n < ring_steps:
                ring_pass(n)
            if what == "add" and n < ring_steps:
                compose([n, nz - n])

    segment = None
    forward = []
    for level in range(levels + 1):
        if level == 0:
            wait_one(0)
            segment = quarter[0]
            forward.append(segment)
            continue
        n = level - 1
        wait_set(n)
        for s in range(ny):
            product = dot(segment, fset[n, s])
            for i in range(rows):
                fsrc[n, s * rows + i] = product[:, i * S:(i + 1) * S].astype(BF16)
        if n == 0:
            pl.semaphore_wait(far_sem, 2)
        for d in z_order:
            target = lax.rem(c + d, nz)
            remote(fsrc.at[n, target], frecv.at[n, d - 1], fs_sem.at[n], fr_sem.at[n], z_peer(d)).start()
        if level == 1:
            wait_one(1)
            wait_one(2)
        if level == 2:
            wait_one(3)
            wg[c] = live(1, dot(segment, dup[1]))
            for d in z_order:
                remote(wg.at[c], wg.at[c], w_send, w_recv, z_peer(d)).start()
        if level == levels:
            wait_set(nset - 1)
        background(level)
        drain(frecv.at[n], fr_sem.at[n])
        total = fsrc[n, c].astype(F32)
        for d in range(1, nz):
            total = total + frecv[n, d - 1].astype(F32)
        if level < levels:
            lowered = (quarter[level].astype(F32) - total).astype(BF16)
            segment = live(level, dot(lowered, dmine[level]))
            forward.append(segment)

    lrecv[k] = total.astype(BF16)
    for d in l_order:
        remote(lrecv.at[k], lrecv.at[k], l_send, l_recv, l_peer(d)).start()
    background(4)
    drain(lrecv.at[pl.ds(0, nl - 1)], l_recv)
    total = lrecv[0].astype(F32)
    for n in range(1, nl):
        total = total + lrecv[n].astype(F32)
    lowered = (quarter[levels].astype(F32) - total).astype(BF16)
    afwd = dot(lowered, dmine[levels]).astype(BF16)
    solved = dot(afwd, dmine[levels + 1]).astype(BF16)

    mine = pl.ds(pl.multiple_of(p * rq, rq), rq)
    sol_copies = []
    anc_copies = []

    def give(level, value):
        osol[0, level, 0, mine] = value
        part = osol.at[0, level, 0, mine]
        for m, d in enumerate(y_order):
            copy = remote(part, part, os_send.at[level, m], os_recv.at[level], y_peer(d))
            copy.start()
            sol_copies.append(copy)

    def spread(step, value):
        ag[step, c] = value
        for d in z_order:
            remote(ag.at[step, c], ag.at[step, c], ag_send.at[step], ag_recv.at[step], z_peer(d)).start()

    def parents(slots, s):
        return jnp.concatenate([slots[s * rows + i] for i in range(rows)], axis=1)

    def sums(slots, blocks):
        total = None
        for s in range(ny):
            product = dot(parents(slots, s), blocks[s])
            total = product if total is None else total + product
        return total

    def finish(level, total):
        lowered = (forward[level].astype(F32) - total).astype(BF16)
        return live(level, dot(lowered, dup[level]))

    spread(0, solved)
    background(5)
    compose([0, nz // 2])
    bset[levels, p] = eacc[...].astype(BF16)
    send_set(composed)
    drain(wg.at[pl.ds(0, nz - 1)], w_recv)
    fixed = sums(wg, bset.at[levels - 1])
    wait_set(levels)
    drain(ag.at[0, pl.ds(0, nz - 1)], ag_recv.at[0])
    top = finish(levels - 1, sums(ag.at[0], bset.at[0]))
    spread(1, top)
    give(levels - 1, top)
    for i in range(rows):
        oanc[i, mine] = ag[0, p * rows + i]
        for m, d in enumerate(y_order):
            theirs = lax.rem(p + d, ny) * rows + i
            copy = remote(ag.at[0, theirs], oanc.at[i, mine], oa_send.at[i, m], oa_recv, y_peer(d))
            copy.start()
            anc_copies.append(copy)
    wait_set(levels + 1)
    wait_set(composed)
    drain(ag.at[1, pl.ds(0, nz - 1)], ag_recv.at[1])
    give(0, finish(0, fixed - sums(ag.at[1], bset.at[levels])))
    give(1, finish(1, sums(ag.at[1], bset.at[1])))

    for level in reversed(range(levels)):
        drain(osol.at[0, level, 0, pl.ds(0, (ny - 1) * rq)], os_recv.at[level])
    drain(oanc.at[:, pl.ds(0, (ny - 1) * rq)], oa_recv)
    for copy in set_copies + sol_copies + anc_copies + ring_copies:
        copy.wait_send()

    @pl.when(owner)
    def _():
        for copies in one_all:
            for copy in copies:
                copy.wait_send()

    for n in range(levels):
        drain(frecv.at[n], fs_sem.at[n])
    for n in range(2):
        drain(ag.at[n, pl.ds(0, nz - 1)], ag_send.at[n])
    drain(wg.at[pl.ds(0, nz - 1)], w_send)
    drain(lrecv.at[pl.ds(0, nl - 1)], l_send)


def per_device(nl, ny, nz, *operands):
    operands = list(operands)
    operands[5] = operands[5].transpose(0, 1, 3, 2)
    operands[6] = operands[6].transpose(1, 0, 2)
    operands[12] = operands[12].transpose(0, 2, 1)
    rhs = operands[0]
    levels, rows, R, S = rhs.shape[1:]
    rq = R // ny
    nset = 2 * levels
    dma = pltpu.SemaphoreType.DMA
    scratch = [
        pltpu.SMEM(operands[5].shape, jnp.int32),
        pltpu.SMEM(operands[12].shape, jnp.int32),
        pltpu.SMEM(operands[6].shape, jnp.int32),
        pltpu.VMEM((nset, rows, S, S), BF16),
        pltpu.VMEM((levels + 2, S, S), BF16),
        pltpu.VMEM((levels + 1, R, S), BF16),
        pltpu.VMEM((R, S), BF16),
        pltpu.VMEM((levels, S, S), BF16),
        pltpu.VMEM((levels + 1, rq, S), BF16),
        pltpu.VMEM((levels, ny, S, rows * S), BF16),
        pltpu.VMEM((levels + 1, ny, rows * S, S), BF16),
        pltpu.VMEM((levels, nz, rq, S), BF16),
        pltpu.VMEM((levels, nz - 1, rq, S), BF16),
        pltpu.VMEM((nl, rq, S), BF16),
        pltpu.VMEM((2, nz, rq, S), BF16),
        pltpu.VMEM((nz, rq, S), BF16),
        pltpu.VMEM((nz, rows * S, S), BF16),
        pltpu.VMEM((rows * S, S), F32),
        dma((4 + nset,)), dma((5,)), pltpu.SemaphoreType.REGULAR,
        dma((nset + 1, ny - 1)), dma((nset + 1,)), dma((4, ny - 1)), dma((4,)),
        dma((levels,)), dma((levels,)), dma, dma, dma((2,)), dma((2,)),
        dma((rows, ny - 1)), dma, dma((levels, ny - 1)), dma((levels,)),
        dma, dma, dma((2, 2, nz // 2)), dma((2, 2, nz // 2)),
    ]
    return pl.pallas_call(
        functools.partial(kernel, nl, ny, nz, levels, rows, rq, S),
        out_shape=(
            jax.ShapeDtypeStruct((1, levels, 1, R, S), BF16),
            jax.ShapeDtypeStruct((rows, R, S), BF16),
        ),
        in_specs=[pl.BlockSpec(memory_space=pl.ANY)] * len(operands),
        out_specs=(pl.BlockSpec(memory_space=pltpu.VMEM),) * 2,
        scratch_shapes=scratch,
        compiler_params=pltpu.CompilerParams(
            collective_id=0, has_side_effects=True, vmem_limit_bytes=60 * 2**20
        ),
        name="solve",
    )(*operands)


def solution(mesh):
    sizes = [mesh.shape[name] for name in ("layer", "prow", "pcol")]
    return jax.shard_map(
        functools.partial(per_device, *sizes),
        mesh=mesh,
        in_specs=(
            P("layer", None, "prow", None, None),
            P("layer", None, "prow", None, None),
            P("layer", None, "pcol", None, None),
            P("layer", None, "prow", "pcol", None, None),
            P("layer", None, "prow", "pcol", None, None),
            P("layer", None, "prow", "pcol"),
            P("layer", None, None),
            P("prow", None, None),
            P("prow", None, None),
            P("prow", None, None),
            P("layer", "prow", "pcol", None, None),
            P("layer", "prow", "pcol", None, None),
            P("layer", "prow", "pcol"),
        ),
        out_specs=(P("layer", None, "pcol", None, None), P("prow", None, None)),
        check_vma=False,
    )
```

```python
import functools

import jax
import jax.numpy as jnp
from jax import lax
from jax.experimental import pallas as pl
from jax.experimental.pallas import tpu as pltpu
from jax.sharding import PartitionSpec as P

MESH = pl.DeviceIdType.MESH
BF16 = jnp.bfloat16
F32 = jnp.float32


def far_first(n):
    return sorted(range(1, n), key=lambda d: (-min(d, n - d), d))


def dot(a, b):
    return jnp.dot(a, b, preferred_element_type=F32)


def kernel(
    nl, ny, nz, levels, rows, rq, S,
    rhs, diag_low, diag_up, low, up, pattern, sizes,
    anc_rhs, anc_dl, anc_du, anc_low, anc_up, anc_pattern,
    osol, oanc,
    pat_v, apat_v, size_v, raw, dmine, rfull, f0, dup, quarter, amat, afull, arhs,
    fset, bset,
    fsrc, frecv, asrc, arecv, lrecv, agx, ag, wg, ring, eacc,
    in_sem, own_sem, anc_in, far_sem, set_send, set_recv, one_send, one_recv, anc_send, anc_recv,
    fs_sem, fr_sem, l_send, l_recv, ag_send, ag_recv, oa_send, oa_recv, os_send, os_recv,
    w_send, w_recv, ring_send, ring_recv,
):
    k = lax.axis_index("layer")
    p = lax.axis_index("prow")
    c = lax.axis_index("pcol")
    j = lax.rem(c, rows)
    owner = p == c // rows
    nset = 2 * levels
    composed = nset
    zh = nz // 2
    g = lax.rem(c, zh)
    ring_steps = nz // 2
    half = rows * S // 2
    y_order, z_order, l_order = far_first(ny), far_first(nz), far_first(nl)

    def y_peer(d):
        return (k, lax.rem(p + d, ny), c)

    def z_peer(d):
        return (k, p, lax.rem(c + d, nz))

    def l_peer(d):
        return (lax.rem(k + d, nl), p, c)

    def drain(ref, sem):
        pltpu.make_async_copy(ref, ref, sem).wait()

    def remote(src, dst, send, recv, device):
        return pltpu.make_async_remote_copy(
            src_ref=src, dst_ref=dst, send_sem=send, recv_sem=recv,
            device_id=device, device_id_type=MESH,
        )

    reach = nz // 4
    near = [d for d in z_order if min(d, nz - d) <= reach]
    barrier = pltpu.get_barrier_semaphore()
    greeted = [z_peer(d) for d in near] + [y_peer(d) for d in y_order] + [l_peer(d) for d in l_order]
    for device in greeted:
        pl.semaphore_signal(barrier, inc=1, device_id=device, device_id_type=MESH)

    def fetch(src, dst, n):
        copy = pltpu.make_async_copy(src, dst, in_sem.at[n])
        copy.start()
        return copy

    sets_in = [low.at[0, l, :, 0] for l in range(levels - 1)] + [anc_low.at[0, :, 0], anc_up.at[0, :, 0]]
    sets_in += [up.at[0, l, :, 0] for l in reversed(range(levels - 1))]
    got_pat = fetch(pattern, pat_v, 0)
    got_apat = fetch(anc_pattern, apat_v, 1)
    got_size = fetch(sizes, size_v, 2)
    got_sets = [fetch(sets_in[0], raw.at[0], 3)]
    own = [
        pltpu.make_async_copy(diag_low.at[0, :, j], dmine.at[pl.ds(0, levels)], own_sem.at[0]),
        pltpu.make_async_copy(rhs.at[0, :, j], rfull.at[pl.ds(0, levels)], own_sem.at[1]),
    ]
    holder = [p == (g + u * zh) // rows for u in range(2)]
    anc_row = [lax.rem(g + u * zh, rows) for u in range(2)]
    anc_own = [
        [
            pltpu.make_async_copy(anc_rhs.at[anc_row[u]], afull.at[u], anc_in.at[u, 0]),
            pltpu.make_async_copy(anc_dl.at[anc_row[u]], amat.at[u, 0], anc_in.at[u, 1]),
            pltpu.make_async_copy(anc_du.at[anc_row[u]], amat.at[u, 1], anc_in.at[u, 2]),
        ]
        for u in range(2)
    ]

    @pl.when(owner)
    def _():
        for copy in own:
            copy.start()

    for u in range(2):
        @pl.when(holder[u])
        def _():
            for copy in anc_own[u]:
                copy.start()

    for n in range(1, nset):
        got_sets.append(fetch(sets_in[n], raw.at[n], 3 + n))
    got_dup = fetch(diag_up.at[0, :, 0], dup, 3 + nset)

    def link(n, i):
        if n < levels - 1:
            return pat_v[0, n, 0, i]
        if n < levels + 1:
            return apat_v[0, 0, i]
        return pat_v[0, nset - 1 - n, 0, i]

    def mask_set(n):
        got_sets[n].wait()
        for i in range(rows):
            present = jnp.full((S, S), link(n, i), jnp.int32).astype(F32).astype(BF16)
            block = raw[n, i] * present
            if n < levels:
                fset[n, p, :, i * S:(i + 1) * S] = block
            else:
                bset[n - levels, p, i * S:(i + 1) * S, :] = block

    set_copies = []

    def send_set(n):
        part = fset.at[n, p] if n < levels else bset.at[n - levels, p]
        for m, d in enumerate(y_order):
            copy = remote(part, part, set_send.at[n, m], set_recv.at[n], y_peer(d))
            copy.start()
            set_copies.append(copy)

    def wait_set(n):
        whole = fset.at[n] if n < levels else bset.at[n - levels]
        drain(whole.at[pl.ds(0, ny - 1)], set_recv.at[n])

    def live(level, value):
        columns = lax.broadcasted_iota(jnp.int32, value.shape, 1)
        return jnp.where(columns < size_v[level, 0, c], value, 0.0).astype(BF16)

    def ring_parts(t, h, move):
        both = [(0, lax.rem(c + nz - t - move, nz), 1), (1, lax.rem(c + t + move, nz), nz - 1)]
        return [both[h]] if t == ring_steps - 1 else both

    ring_copies = []

    def ring_start(t, h):
        for m, slot, d in ring_parts(t, h, 0):
            block = ring.at[slot, pl.ds(h * half, half)]
            copy = remote(block, block, ring_send.at[m, h, t], ring_recv.at[m, h, t], z_peer(d))
            copy.start()
            ring_copies.append(copy)

    def ring_pass(t):
        for h in range(2):
            for m, slot, d in ring_parts(t, h, 1):
                drain(ring.at[slot, pl.ds(h * half, half)], ring_recv.at[m, h, t])
            if t + 1 < ring_steps:
                ring_start(t + 1, h)

    def up0(slot):
        row = pl.ds(pl.multiple_of(lax.rem(slot, rows) * S, S), S)
        return bset[levels - 1, slot // rows, row, :]

    def compose(offsets):
        slots = [lax.rem(c + o, nz) for o in offsets]
        left = jnp.concatenate([ring[slot] for slot in slots], axis=1)
        right = jnp.concatenate([up0(slot) for slot in slots], axis=0)
        eacc[...] += dot(left, right)

    got_pat.wait()
    got_apat.wait()
    got_size.wait()
    mask_set(0)

    @pl.when(owner)
    def _():
        for copy in own:
            copy.wait()
        f0[...] = live(0, dot(rfull[0], dmine[0]))
        mine = pl.ds(pl.multiple_of(p * rq, rq), rq)
        quarter[0] = f0[mine]
        for n in range(1, levels):
            quarter[n] = rfull[n, mine]

    eacc[...] = jnp.zeros_like(eacc)
    mask_set(levels + 1)
    got_dup.wait()
    ring[c] = live(1, dot(bset[1, p], dup[1]))
    pl.semaphore_wait(barrier, len(greeted))
    for d in (reach, nz - reach):
        pl.semaphore_signal(far_sem, inc=1, device_id=z_peer(d), device_id_type=MESH)

    def one_copies(m, d):
        theirs = pl.ds(pl.multiple_of(lax.rem(p + d, ny) * rq, rq), rq)
        pairs = [
            (f0.at[theirs], quarter.at[0]),
            (rfull.at[pl.ds(1, levels - 1), theirs], quarter.at[pl.ds(1, levels - 1)]),
            (dmine.at[1], dmine.at[1]),
            (dmine.at[pl.ds(2, levels - 2)], dmine.at[pl.ds(2, levels - 2)]),
        ]
        return [
            remote(src, dst, one_send.at[n, m], one_recv.at[n], y_peer(d))
            for n, (src, dst) in enumerate(pairs)
        ]

    one_all = [one_copies(m, d) for m, d in enumerate(y_order)]

    def send_one(n):
        @pl.when(owner)
        def _():
            for copies in one_all:
                copies[n].start()

    def wait_one(n):
        @pl.when(jnp.logical_not(owner))
        def _():
            one_all[0][n].wait_recv()

    send_one(0)
    send_set(0)
    ring_start(0, 0)
    ring_start(0, 1)
    send_one(1)
    send_one(2)
    mask_set(1)
    send_set(1)

    send_one(3)

    def anc_copies_of(u, m, d):
        theirs = pl.ds(pl.multiple_of(lax.rem(p + d, ny) * rq, rq), rq)
        return [
            remote(afull.at[u, theirs], arhs.at[u], anc_send.at[u, 0, m], anc_recv.at[u, 0], y_peer(d)),
            remote(amat.at[u], amat.at[u], anc_send.at[u, 1, m], anc_recv.at[u, 1], y_peer(d)),
        ]

    anc_given = [[anc_copies_of(u, m, d) for m, d in enumerate(y_order)] for u in range(2)]

    mask_set(2)
    send_set(2)
    for u in range(2):
        @pl.when(holder[u])
        def _():
            for copy in anc_own[u]:
                copy.wait()
            arhs[u] = afull[u, pl.ds(pl.multiple_of(p * rq, rq), rq)]
            for copies in anc_given[u]:
                for copy in copies:
                    copy.start()

    for n in [nset - 1, levels, levels + 1]:
        if n != levels + 1:
            mask_set(n)
        send_set(n)
    ring_pass(0)
    if ring_steps > 1:
        ring_pass(1)

    plan = {
        1: [("step", 2)],
        2: [("step", 3)],
        3: [("step", 4), ("add", 1), ("add", 2), ("add", 3), ("add", 4)],
        4: [("step", 5)],
        5: [("step", 6), ("add", 5), ("add", 6)],
        6: [("step", 7), ("add", 7)],
    }

    def background(phase):
        for what, n in plan[phase]:
            if what == "step" and n < ring_steps:
                ring_pass(n)
            if what == "add" and n < ring_steps:
                compose([n, nz - n])

    segment = None
    forward = []
    for level in range(levels + 1):
        if level == 0:
            wait_one(0)
            segment = quarter[0]
            forward.append(segment)
            continue
        n = level - 1
        wait_set(n)
        for s in range(ny):
            product = dot(segment, fset[n, s])
            for i in range(rows):
                piece = product[:, i * S:(i + 1) * S].astype(BF16)
                row = s * rows + i
                if level < levels:
                    fsrc[n, row] = piece
                else:
                    asrc[row % zh, row // zh] = piece
        if n == 0:
            pl.semaphore_wait(far_sem, 2)
        for d in z_order:
            target = lax.rem(c + d, nz)
            if level < levels:
                src, dst = fsrc.at[n, target], frecv.at[n, d - 1]
            else:
                src, dst = asrc.at[lax.rem(target, zh)], arecv.at[c]
            remote(src, dst, fs_sem.at[n], fr_sem.at[n], z_peer(d)).start()
        if level == 1:
            wait_one(1)
            wait_one(2)
        if level == 2:
            wait_one(3)
            wg[c] = live(1, dot(segment, dup[1]))
            for d in z_order:
                remote(wg.at[c], wg.at[c], w_send, w_recv, z_peer(d)).start()
        if level == levels:
            wait_set(nset - 1)
        background(level)
        if level == levels:
            break
        drain(frecv.at[n], fr_sem.at[n])
        total = fsrc[n, c].astype(F32)
        for d in range(1, nz):
            total = total + frecv[n, d - 1].astype(F32)
        lowered = (quarter[level].astype(F32) - total).astype(BF16)
        segment = live(level, dot(lowered, dmine[level]))
        forward.append(segment)

    arecv[c] = asrc[g]
    drain(arecv.at[pl.ds(0, nz - 1)], fr_sem.at[levels - 1])
    total = arecv[0].astype(F32)
    for n in range(1, nz):
        total = total + arecv[n].astype(F32)
    lrecv[k] = total.astype(BF16)
    for d in l_order:
        remote(lrecv.at[k], lrecv.at[k], l_send, l_recv, l_peer(d)).start()
    background(4)
    for u in range(2):
        @pl.when(jnp.logical_not(holder[u]))
        def _():
            for copy in anc_given[u][0]:
                copy.wait_recv()
    drain(lrecv.at[pl.ds(0, nl - 1)], l_recv)
    total = lrecv[0].astype(F32)
    for n in range(1, nl):
        total = total + lrecv[n].astype(F32)
    for u in range(2):
        lowered = (arhs[u].astype(F32) - total[u]).astype(BF16)
        afwd = dot(lowered, amat[u, 0]).astype(BF16)
        agx[g, u] = dot(afwd, amat[u, 1]).astype(BF16)

    mine = pl.ds(pl.multiple_of(p * rq, rq), rq)
    sol_copies = []
    anc_copies = []

    def give(level, value):
        osol[0, level, 0, mine] = value
        part = osol.at[0, level, 0, mine]
        for m, d in enumerate(y_order):
            copy = remote(part, part, os_send.at[level, m], os_recv.at[level], y_peer(d))
            copy.start()
            sol_copies.append(copy)

    def sums(slots, blocks):
        total = None
        for s in range(ny):
            product = dot(jnp.concatenate(slots[s * rows:(s + 1) * rows], axis=1), blocks[s])
            total = product if total is None else total + product
        return total

    def finish(level, total):
        lowered = (forward[level].astype(F32) - total).astype(BF16)
        return live(level, dot(lowered, dup[level]))

    part = agx.at[g]
    for d in sorted([d for d in range(1 - zh // 2, zh // 2 + 1) if d], key=lambda d: -abs(d)):
        remote(part, part, ag_send.at[0], ag_recv.at[0], z_peer(d % nz)).start()
    background(5)
    wait_set(levels)
    drain(agx.at[pl.ds(0, zh - 1)], ag_recv.at[0])
    top = finish(levels - 1, sums([agx[a % zh, a // zh] for a in range(nz)], bset.at[0]))
    ag[c] = top
    for d in z_order:
        remote(ag.at[c], ag.at[c], ag_send.at[1], ag_recv.at[1], z_peer(d)).start()
    background(6)
    compose([0, nz // 2])
    bset[levels, p] = eacc[...].astype(BF16)
    send_set(composed)
    give(levels - 1, top)
    for i in range(rows):
        row = p * rows + i
        oanc[i, mine] = agx[lax.rem(row, zh), row // zh]
        for m, d in enumerate(y_order):
            theirs = lax.rem(p + d, ny) * rows + i
            copy = remote(
                agx.at[lax.rem(theirs, zh), theirs // zh], oanc.at[i, mine], oa_send.at[i, m], oa_recv, y_peer(d),
            )
            copy.start()
            anc_copies.append(copy)
    drain(wg.at[pl.ds(0, nz - 1)], w_recv)
    fixed = sums([wg[i] for i in range(nz)], bset.at[levels - 1])
    wait_set(levels + 1)
    drain(ag.at[pl.ds(0, nz - 1)], ag_recv.at[1])
    slots = [ag[i] for i in range(nz)]
    second = finish(1, sums(slots, bset.at[1]))
    wait_set(composed)
    give(0, finish(0, fixed - sums(slots, bset.at[levels])))
    give(1, second)

    for level in reversed(range(levels)):
        drain(osol.at[0, level, 0, pl.ds(0, (ny - 1) * rq)], os_recv.at[level])
    drain(oanc.at[:, pl.ds(0, (ny - 1) * rq)], oa_recv)
    for copy in set_copies + sol_copies + anc_copies + ring_copies:
        copy.wait_send()

    @pl.when(owner)
    def _():
        for copies in one_all:
            for copy in copies:
                copy.wait_send()

    for u in range(2):
        @pl.when(holder[u])
        def _():
            for copies in anc_given[u]:
                for copy in copies:
                    copy.wait_send()

    for n in range(levels - 1):
        drain(frecv.at[n], fs_sem.at[n])
    drain(arecv.at[pl.ds(0, nz - 1)], fs_sem.at[levels - 1])
    drain(agx.at[pl.ds(0, zh - 1)], ag_send.at[0])
    drain(ag.at[pl.ds(0, nz - 1)], ag_send.at[1])
    drain(wg.at[pl.ds(0, nz - 1)], w_send)
    drain(lrecv.at[pl.ds(0, nl - 1)], l_send)


def per_device(nl, ny, nz, *operands):
    operands = list(operands)
    operands[5] = operands[5].transpose(0, 1, 3, 2)
    operands[6] = operands[6].transpose(1, 0, 2)
    operands[12] = operands[12].transpose(0, 2, 1)
    rhs = operands[0]
    levels, rows, R, S = rhs.shape[1:]
    rq = R // ny
    nset = 2 * levels
    dma = pltpu.SemaphoreType.DMA
    scratch = [
        pltpu.SMEM(operands[5].shape, jnp.int32),
        pltpu.SMEM(operands[12].shape, jnp.int32),
        pltpu.SMEM(operands[6].shape, jnp.int32),
        pltpu.VMEM((nset, rows, S, S), BF16),
        pltpu.VMEM((levels, S, S), BF16),
        pltpu.VMEM((levels, R, S), BF16),
        pltpu.VMEM((R, S), BF16),
        pltpu.VMEM((levels, S, S), BF16),
        pltpu.VMEM((levels, rq, S), BF16),
        pltpu.VMEM((2, 2, S, S), BF16),
        pltpu.VMEM((2, R, S), BF16),
        pltpu.VMEM((2, rq, S), BF16),
        pltpu.VMEM((levels, ny, S, rows * S), BF16),
        pltpu.VMEM((levels + 1, ny, rows * S, S), BF16),
        pltpu.VMEM((levels - 1, nz, rq, S), BF16),
        pltpu.VMEM((levels - 1, nz - 1, rq, S), BF16),
        pltpu.VMEM((nz // 2, 2, rq, S), BF16),
        pltpu.VMEM((nz, 2, rq, S), BF16),
        pltpu.VMEM((nl, 2, rq, S), BF16),
        pltpu.VMEM((nz // 2, 2, rq, S), BF16),
        pltpu.VMEM((nz, rq, S), BF16),
        pltpu.VMEM((nz, rq, S), BF16),
        pltpu.VMEM((nz, rows * S, S), BF16),
        pltpu.VMEM((rows * S, S), F32),
        dma((4 + nset,)), dma((2,)), dma((2, 3)), pltpu.SemaphoreType.REGULAR,
        dma((nset + 1, ny - 1)), dma((nset + 1,)), dma((4, ny - 1)), dma((4,)),
        dma((2, 2, ny - 1)), dma((2, 2)),
        dma((levels,)), dma((levels,)), dma, dma, dma((2,)), dma((2,)),
        dma((rows, ny - 1)), dma, dma((levels, ny - 1)), dma((levels,)),
        dma, dma, dma((2, 2, nz // 2)), dma((2, 2, nz // 2)),
    ]
    return pl.pallas_call(
        functools.partial(kernel, nl, ny, nz, levels, rows, rq, S),
        out_shape=(
            pltpu.VMEM((1, levels, 1, R, S), BF16),
            pltpu.VMEM((rows, R, S), BF16),
        ),
        in_specs=[pl.BlockSpec(memory_space=pl.ANY)] * len(operands),
        out_specs=(pl.BlockSpec(memory_space=pltpu.VMEM),) * 2,
        scratch_shapes=scratch,
        compiler_params=pltpu.CompilerParams(
            collective_id=0, has_side_effects=True, vmem_limit_bytes=60 * 2**20
        ),
        name="solve",
    )(*operands)


def solution(mesh):
    sizes = [mesh.shape[name] for name in ("layer", "prow", "pcol")]
    return jax.shard_map(
        functools.partial(per_device, *sizes),
        mesh=mesh,
        in_specs=(
            P("layer", None, "prow", None, None),
            P("layer", None, "prow", None, None),
            P("layer", None, "pcol", None, None),
            P("layer", None, "prow", "pcol", None, None),
            P("layer", None, "prow", "pcol", None, None),
            P("layer", None, "prow", "pcol"),
            P("layer", None, None),
            P("prow", None, None),
            P("prow", None, None),
            P("prow", None, None),
            P("layer", "prow", "pcol", None, None),
            P("layer", "prow", "pcol", None, None),
            P("layer", "prow", "pcol"),
        ),
        out_specs=(P("layer", None, "pcol", None, None), P("prow", None, None)),
        check_vma=False,
    )
```
